32 devices in a mesh: seq: 4 (over x, core), tp: 8 (over z, y).
Axes of the slice: x: 2, y: 2, z: 4, core: 2. Of those that a mesh axis runs over, the one named last changes fastest.
Arguments:
- tokens: bfloat16 [1024, 5120], P('seq', 'tp'), may hold values from -6 to 6
- norm_gain: float32 [5120], replicated, may hold values from 0.1 to 1.9
- q_weight: bfloat16 [5120, 5120], P(None, 'tp'), may hold values from -0.078125 to 0.078125
- kv_weight: bfloat16 [5120, 2, 1024], P(None, None, 'tp'), may hold values from -0.078125 to 0.078125
- out_weight: bfloat16 [5120, 5120], P('tp'), may hold values from -0.5 to 0.5
- ctx_cache: bfloat16 [4096, 2, 1024], P('seq', None, 'tp'), may hold values from -1000 to 1000, as said below
- span_start: int32 [1], replicated, may hold values from 1024 to 4096
- finished_cache: bfloat16 [4, 4096, 2, 1024], P(None, 'seq', None, 'tp'), may hold values from -6 to 6
- block_dest: int32 [256, 1], P('seq'), may hold values from 0 to 3; in each aligned block of 64 rows (0 to 63, 64 to 127, ...) at most 32 rows name the same one
Outputs:
- attended: bfloat16 [1024, 5120], P('seq', 'tp')
- page_pool: bfloat16 [4, 8192, 2, 1024], P(None, 'seq', None, 'tp')
The draws below stay inside these ranges and needn't reach their ends.
Inputs may be any that keep to these rules, and one draw needn't show every extreme that they name: `block_dest`: among the 64 blocks of one index of seq, no decode index is named more than 32 times, and some decode index is named exactly 32 times. `ctx_cache`: keys are stored already rotated at their positions; keys may reach some hundreds in magnitude, values lie within -6 to 6.
All inputs are finite; a program needn't handle non-finite values.
Results may differ from the reference program's by a relative error of at most 0.03.
The reference program's roundings to bfloat16 on the way (of `normed`, `queries`, `rounded` and `mixed_heads`) count: a program that leaves them out, or rounds other values in their place, can miss the bound.
Values may be sent and summed in bfloat16 or wider, within the bound.
A program may use at most 128 MiB of HBM per device.

```python
import math
import jax
import jax.numpy as jnp
import numpy as np
from jax import lax

D = 5120
HQ = 40
KVH = 8
HD = 128
TOK_DEV = 256
LAYERS = 4
BLK = 16
TOKENS = 1024
CTX = 4096
FIN = 4096
BLK_DEV = 64
NBLK = 256
CAP = 32
POOL = 8192
N_SEQ = 4


def draw_ctx_cache(key, part):
    drawn = jnp.clip(jax.random.normal(key, (CTX, 2, KVH * HD), jnp.float32), -6.0, 6.0)
    return drawn.astype(jnp.bfloat16)


def levels(rng, dims, pieces, smallest, top_value):
    factor_of = 1.0
    for dim, blocks in pieces:
        steps = jax.random.uniform(jax.random.fold_in(jax.random.fold_in(rng, 6), dim), (blocks,), jnp.float32, smallest / len(pieces), top_value / len(pieces))
        factor_of = factor_of * jnp.repeat(jnp.exp(steps), dims[dim] // blocks).reshape((-1,) + (1,) * (len(dims) - 1 - dim))
    return factor_of


def deal_out(rng, own, number, rows, amount, top, reach, slope):
    ranking = jax.random.permutation(rng, amount)
    packed, common = portions_of(amount, rows * top, reach, slope, True), portions_of(amount, rows * top, reach, slope, False)
    places = jnp.arange(amount)

    def named(sizes, offset_by):
        used = int((sizes > 0).sum())
        fixed = max(1, used // 4)
        shifted = fixed + (places - fixed + offset_by * (used - fixed)) % max(1, amount - fixed)
        return jnp.zeros((amount,), jnp.int32).at[ranking[jnp.where(places < fixed, places, shifted)]].set(jnp.asarray(sizes, jnp.int32))

    sizes = jnp.where(number % 4 == 0, named(packed, number // 4), named(common, number - number // 4 - 1))
    mixed = jax.random.permutation(jax.random.fold_in(own, 3), amount)
    giver, receiver = mixed[0:amount // 2 * 2:2], mixed[1:amount // 2 * 2:2]
    room = jnp.minimum(sizes[giver] - 1, reach - sizes[receiver]) // 2
    room = jnp.where((giver == ranking[0]) | (receiver == ranking[0]) | (sizes[receiver] == 0), 0, jnp.maximum(room, 0))
    shifted = jax.random.randint(jax.random.fold_in(own, 4), (amount // 2,), 0, 1 << 20) % (room + 1)
    sizes = sizes.at[giver].add(-shifted).at[receiver].add(shifted)
    labels = jnp.searchsorted(jnp.cumsum(sizes), jnp.arange(rows * top), side="right").astype(jnp.int32)
    table = labels.reshape(top, rows).T
    table = table[jax.random.permutation(jax.random.fold_in(own, 1), rows)]
    offset_by = jax.random.randint(jax.random.fold_in(own, 2), (rows, 1), 0, top)
    return jnp.take_along_axis(table, (jnp.arange(top)[None, :] + offset_by) % top, axis=1)


def portions_of(amount, total, bound, slope, full):
    loads = [(1 << 20) // math.isqrt(standing ** slope) + 1 for standing in range(1, amount + 1)]
    largest = bound if full else min(bound, max(-(-total // amount), total * loads[0] // sum(loads)))
    least = 1 if total - largest >= amount - 1 else 0
    counts, spare = [largest] + [least] * (amount - 1), total - largest - least * (amount - 1)
    while spare > 0:
        movable = [i for i in range(1, amount) if counts[i] < largest] or [i for i in range(1, amount) if counts[i] < bound]
        pool, left = sum([loads[i] for i in movable]), spare
        for i in movable:
            addition = min(bound - counts[i], max(1, left * loads[i] // pool), spare)
            counts[i] = counts[i] + addition
            spare = spare - addition
    return np.array(counts)


def normal_values(key, shape, deviation, limit, pieces=(), held_as=jnp.bfloat16):
    entries = jax.random.normal(key, shape, jnp.float32) * deviation
    if len(pieces) > 0:
        entries = levels(key, shape, pieces, -0.22, 0.18) * entries
    return jnp.clip(entries, min=-limit, max=limit).astype(held_as)


def setup_inputs(seed: int = 0) -> dict:
    key_of = jax.random.split(jax.random.key(seed), 10)
    tokens = normal_values(key_of[0], (TOKENS, D), 1.0, 6.0, ((0, 4), (1, 8)))
    norm_gain = jnp.clip(1.0 + 0.18 * jax.random.normal(key_of[1], (D,), jnp.float32), 0.1, 1.9)
    q_weight = normal_values(key_of[2], (D, HQ * HD), D ** -0.5, 0.078125, ((1, 8),))
    kv_weight = normal_values(key_of[3], (D, 2, KVH * HD), D ** -0.5, 0.078125, ((2, 8),))
    out_weight = normal_values(key_of[4], (HQ * HD, D), HD ** -0.5, 0.5, ((0, 8),))
    ctx_cache = draw_ctx_cache(jax.random.fold_in(key_of[9], 71), 0)
    span_start = jax.random.randint(key_of[6], (1,), CTX // 4, CTX + 1).astype(jnp.int32)
    finished_cache = normal_values(key_of[7], (LAYERS, FIN, 2, KVH * HD), 1.0, 6.0, ((1, 4), (3, 8)))
    block_dest_keys = jax.random.split(jax.random.fold_in(key_of[8], 1), NBLK // BLK_DEV)
    block_dest_turns = jax.random.permutation(jax.random.fold_in(key_of[8], 3), NBLK // BLK_DEV)
    block_dest = jax.vmap(lambda own, number: deal_out(jax.random.fold_in(key_of[8], 2), own, number, BLK_DEV, N_SEQ, 1, CAP, 2))(block_dest_keys, block_dest_turns).reshape((NBLK, 1))
    return dict(tokens=tokens, norm_gain=norm_gain, q_weight=q_weight, kv_weight=kv_weight, out_weight=out_weight, ctx_cache=ctx_cache, span_start=span_start, finished_cache=finished_cache, block_dest=block_dest)


rms_eps = 1e-06
rope_base = 1000000.0
neg_fill = -1e+30

def rotate_pairs(values, positions):
    half_width = values.shape[-1] // 2
    frequency = jnp.exp(jnp.arange(half_width, dtype=jnp.float32) * (-2.0 * math.log(rope_base) / values.shape[-1]))
    angles = positions[:, None] * frequency[None, :]
    cosine = jnp.cos(angles)[:, None, :]
    sine_part = jnp.sin(angles)[:, None, :]
    first_half = values[..., :half_width]
    second_half = values[..., half_width:]
    return jnp.concatenate([first_half * cosine - second_half * sine_part, second_half * cosine + first_half * sine_part], -1)

def reference(tokens, norm_gain, q_weight, kv_weight, out_weight, ctx_cache, span_start, finished_cache, block_dest):
    head_group = HQ // KVH
    widened = tokens.astype(jnp.float32)
    normed = (widened * lax.rsqrt(lax.optimization_barrier(jnp.mean(widened * widened, axis=-1, keepdims=True)) + rms_eps) * norm_gain).astype(jnp.bfloat16)
    span_first = span_start[0]
    positions = (span_first + jnp.arange(TOKENS, dtype=jnp.int32)).astype(jnp.float32)
    queries = jnp.dot(normed, q_weight, preferred_element_type=jnp.float32).reshape(TOKENS, HQ, HD)
    queries = rotate_pairs(queries, positions).astype(jnp.bfloat16).reshape(TOKENS, KVH, head_group, HD)
    queries = lax.optimization_barrier(queries)
    projected = jnp.dot(normed, kv_weight.reshape(D, 2 * KVH * HD), preferred_element_type=jnp.float32).reshape(TOKENS, 2, KVH, HD)
    new_keys = rotate_pairs(projected[:, 0], positions).astype(jnp.bfloat16)
    new_values = projected[:, 1].astype(jnp.bfloat16)
    all_keys = jnp.concatenate([ctx_cache[:, 0].reshape(CTX, KVH, HD), new_keys], 0)
    all_values = jnp.concatenate([ctx_cache[:, 1].reshape(CTX, KVH, HD), new_values], 0)
    all_keys, all_values = lax.optimization_barrier((all_keys, all_values))
    cached_visible = jnp.arange(CTX, dtype=jnp.int32) < span_first
    span_order = jnp.arange(TOKENS, dtype=jnp.int32)

    def query_block(block_index):
        block_queries = lax.dynamic_slice_in_dim(queries, block_index * TOK_DEV, TOK_DEV, 0)
        query_order = block_index * TOK_DEV + jnp.arange(TOK_DEV, dtype=jnp.int32)
        visible = jnp.concatenate([jnp.broadcast_to(cached_visible[None, :], (TOK_DEV, CTX)), span_order[None, :] <= query_order[:, None]], 1)

        def one_head(head_index):
            head_queries = lax.dynamic_index_in_dim(block_queries, head_index, 1, keepdims=False).astype(jnp.float32)
            head_keys = lax.dynamic_index_in_dim(all_keys, head_index, 1, keepdims=False).astype(jnp.float32)
            head_values = lax.dynamic_index_in_dim(all_values, head_index, 1, keepdims=False).astype(jnp.float32)
            scores = jnp.einsum('tgd,sd->tgs', head_queries, head_keys) * HD ** (-0.5)
            visible_mask = visible[:, None, :]
            row_max = lax.optimization_barrier(jnp.max(jnp.where(visible_mask, scores, neg_fill), -1, keepdims=True))
            weights = jnp.where(visible_mask, jnp.exp(scores - row_max), 0.0)
            row_total = lax.optimization_barrier(jnp.sum(weights, -1))
            rounded = lax.optimization_barrier(weights.astype(jnp.bfloat16)).astype(jnp.float32)
            summed = jnp.einsum('tgs,sd->tgd', rounded, head_values)
            return (summed / row_total[..., None]).astype(jnp.bfloat16)
        per_head = lax.map(one_head, jnp.arange(KVH, dtype=jnp.int32))
        return jnp.transpose(per_head, (1, 0, 2, 3)).reshape(TOK_DEV, HQ * HD)
    mixed_heads = lax.map(query_block, jnp.arange(N_SEQ, dtype=jnp.int32)).reshape(TOKENS, HQ * HD)
    attended = jnp.dot(mixed_heads, out_weight, preferred_element_type=jnp.float32).astype(jnp.bfloat16)
    destination = block_dest[:, 0].reshape(N_SEQ, BLK_DEV)
    onehot = (destination[:, :, None] == jnp.arange(N_SEQ, dtype=jnp.int32)[None, None, :]).astype(jnp.int32)
    earlier_count = lax.optimization_barrier(jnp.sum((jnp.cumsum(onehot, axis=1, dtype=jnp.int32) - onehot) * onehot, axis=-1))
    source_index = jnp.arange(N_SEQ, dtype=jnp.int32)[:, None]
    target = (destination * (N_SEQ * CAP) + source_index * CAP + earlier_count).reshape(NBLK)
    blocks = finished_cache.reshape(LAYERS, NBLK, BLK, 2, KVH * HD)
    page_pool = jnp.zeros((LAYERS, N_SEQ * N_SEQ * CAP, BLK, 2, KVH * HD), finished_cache.dtype).at[:, target].set(blocks)
    page_pool = page_pool.reshape(LAYERS, POOL, 2, KVH * HD)
    return (attended, page_pool)
```

```python
import functools
import math

import jax
import jax.numpy as jnp
from jax import lax
from jax.experimental import pallas as pl
from jax.experimental.pallas import tpu as pltpu
from jax.sharding import PartitionSpec as P

D = 5120
HD = 128
LAYERS = 4
BLK = 16
NZ = 4

rms_eps = 1e-06
rope_base = 1000000.0
neg_fill = -1e30
MESH = pl.DeviceIdType.MESH


def layer_kernel(
    n_seq, tokens, gain, qw, kvw, ow, ctx, cosf, sinf, span, fin, bdc, bdr,
    att, fin_all, map_all,
    tok, wq, wkv, wo, ctxb, newb, mapb, qacc, kvacc, queries, m_s, l_s, acc_s, mixed,
    ysend, yrecv, zsend, zrecv,
    wsem, lsem, tz_s, tz_r, ty_s, ty_r, cx_s, cx_r, cs_s, cs_r, nx_s, nx_r, ns_s, ns_r,
    fx_s, fx_r, fs_s, fs_r, mx_s, mx_r, ms_s, ms_r, ry_s, ry_r, rz_s, rz_r,
):
    s = lax.axis_index("seq")
    t = lax.axis_index("tp")
    z, y = t // 2, t % 2
    chip, core = s // 2, s % 2
    chips = n_seq // 2
    rows, width = tokens.shape
    heads = width // HD
    ctx_rows = ctx.shape[0]

    def z_peer(k):
        return {"tp": lax.rem(z + k, NZ) * 2 + y}

    y_peer = {"tp": z * 2 + 1 - y}
    sibling = {"seq": chip * 2 + 1 - core}

    def x_peer(k):
        return {"seq": lax.rem(chip + k, chips) * 2 + core}

    def x_source(k):
        return lax.rem(chip + chips - k, chips) * 2 + core

    def remote(src, dst, ssem, rsem, device):
        return pltpu.make_async_remote_copy(
            src_ref=src, dst_ref=dst, send_sem=ssem, recv_sem=rsem,
            device_id=device, device_id_type=MESH,
        )

    loads = [
        pltpu.make_async_copy(qw, wq, wsem.at[0]),
        pltpu.make_async_copy(kvw, wkv, wsem.at[1]),
        pltpu.make_async_copy(ow, wo, wsem.at[2]),
    ]

    barrier = pltpu.get_barrier_semaphore()
    peers = [z_peer(k) for k in range(1, NZ)] + [y_peer, sibling]
    peers += [x_peer(k) for k in range(1, chips)]
    for peer in peers:
        pl.semaphore_signal(barrier, inc=1, device_id=peer, device_id_type=MESH)
    pl.semaphore_wait(barrier, len(peers))

    tz = [
        remote(tokens, tok.at[k], tz_s.at[k], tz_r.at[k], z_peer(k)) for k in range(1, NZ)
    ]
    ty = [remote(tokens, tok.at[NZ], ty_s.at[0], ty_r.at[0], y_peer)]
    ty[0].start()
    for c in tz:
        c.start()

    cx = [
        remote(ctx, ctxb.at[s], cx_s.at[k], cx_r.at[k], x_peer(k)) for k in range(1, chips)
    ]
    for c in cx:
        c.start()
    cs = [remote(ctx, ctxb.at[s], cs_s.at[0], cs_r.at[0], sibling)]
    cs[0].start()
    for w in loads:
        w.start()
    local_ctx = pltpu.make_async_copy(ctx, ctxb.at[s], lsem.at[0])
    local_ctx.start()

    fx = [
        remote(fin, fin_all.at[s], fx_s.at[k], fx_r.at[k], x_peer(k)) for k in range(1, chips)
    ]
    for c in fx:
        c.start()
    fs = [remote(fin, fin_all.at[s], fs_s.at[0], fs_r.at[0], sibling)]
    fs[0].start()
    local_fin = pltpu.make_async_copy(fin, fin_all.at[s], lsem.at[1])
    local_fin.start()

    blocks = bdc.shape[0]
    capacity = 2 * blocks // n_seq
    slots = n_seq * capacity
    earlier = (
        lax.broadcasted_iota(jnp.int32, (blocks, blocks), 1)
        < lax.broadcasted_iota(jnp.int32, (blocks, blocks), 0)
    )
    same = bdr[...] == bdc[...]
    rank = jnp.sum(jnp.where(earlier & same, 1.0, 0.0), axis=1, keepdims=True).astype(jnp.int32)
    slot = bdc[...] * capacity + rank
    match = slot == lax.broadcasted_iota(jnp.int32, (blocks, slots), 1)
    numbers = lax.broadcasted_iota(jnp.int32, (blocks, slots), 0).astype(jnp.float32) + 1.0
    source = jnp.sum(jnp.where(match, numbers, 0.0), axis=0, keepdims=True).astype(jnp.int32) - 1
    mapb[...] = jnp.broadcast_to(source, mapb.shape)
    mx = [
        remote(mapb, map_all.at[s], mx_s.at[k], mx_r.at[k], x_peer(k)) for k in range(1, chips)
    ]
    for c in mx:
        c.start()
    ms = [remote(mapb, map_all.at[s], ms_s.at[0], ms_r.at[0], sibling)]
    ms[0].start()
    local_map = pltpu.make_async_copy(mapb, map_all.at[s], lsem.at[2])
    local_map.start()

    tok[0] = tokens[...]

    for k in range(1, NZ):
        tz[k - 1].wait_recv()
        c = remote(tok.at[k], tok.at[NZ + k], ty_s.at[k], ty_r.at[k], y_peer)
        c.start()
        ty.append(c)
    for k in range(1, chips):
        cx[k - 1].wait_recv()
        src = x_source(k)
        c = remote(ctxb.at[src], ctxb.at[src], cs_s.at[k], cs_r.at[k], sibling)
        c.start()
        cs.append(c)
    for c in ty:
        c.wait_recv()

    def squares(k, total):
        x = tok[k].astype(jnp.float32)
        return total + jnp.sum(x * x, axis=1, keepdims=True)

    total = lax.fori_loop(0, 2 * NZ, squares, jnp.zeros((rows, 1), jnp.float32))
    scale = lax.rsqrt(total / D + rms_eps)
    qacc[...] = jnp.zeros_like(qacc)
    kvacc[...] = jnp.zeros_like(kvacc)
    loads[0].wait()
    loads[1].wait()

    def project(k, carry):
        owner = lax.rem(z + NZ - lax.rem(k, NZ), NZ) * 2 + lax.rem(y + k // NZ, 2)
        x = tok[k].astype(jnp.float32)
        normed = (x * scale * gain[owner]).astype(jnp.bfloat16)
        part = pl.ds(pl.multiple_of(owner * width, HD), width)
        kvacc[...] += jnp.dot(normed, wkv[part, :], preferred_element_type=jnp.float32)
        qacc[...] += jnp.dot(normed, wq[part, :], preferred_element_type=jnp.float32)
        return carry

    lax.fori_loop(0, 2 * NZ, project, 0)
    cosine, sine = cosf[...], sinf[...]

    def rotate(x):
        return (x * cosine + pltpu.roll(x, HD // 2, 1) * sine).astype(jnp.bfloat16)

    newb[s, :, 0:HD] = rotate(kvacc[:, 0:HD])
    newb[s, :, HD : 2 * HD] = kvacc[:, HD : 2 * HD].astype(jnp.bfloat16)
    nx = [
        remote(newb.at[s], newb.at[s], nx_s.at[k], nx_r.at[k], x_peer(k)) for k in range(1, chips)
    ]
    for c in nx:
        c.start()
    ns = [remote(newb.at[s], newb.at[s], ns_s.at[0], ns_r.at[0], sibling)]
    ns[0].start()
    for h in range(heads):
        queries[h] = rotate(qacc[:, h * HD : (h + 1) * HD])

    local_ctx.wait()
    for c in cs:
        c.wait_recv()

    factor = HD**-0.5 * math.log2(math.e)
    span_first = span[0]

    def update(state, q, keys, values, mask):
        row_max, row_total, summed = state
        scores = mask(
            lax.dot_general(
                q, keys, (((1,), (1,)), ((), ())), preferred_element_type=jnp.float32
            )
            * factor
        )
        new_max = jnp.maximum(row_max, jnp.max(scores, axis=1, keepdims=True))
        weights = jnp.exp2(scores - new_max)
        rescale = jnp.exp2(row_max - new_max)
        return (
            new_max,
            row_total * rescale + jnp.sum(weights, axis=1, keepdims=True),
            summed * rescale
            + jnp.dot(
                weights.astype(jnp.bfloat16), values, preferred_element_type=jnp.float32
            ),
        )

    def cached_head(h, carry):
        q = queries[h]

        def step(i, state):
            place = i * ctx_rows + lax.broadcasted_iota(jnp.int32, (1, ctx_rows), 1)
            bias = jnp.where(place < span_first, 0.0, neg_fill)
            return update(
                state, q, ctxb[i, :, 0:HD], ctxb[i, :, HD : 2 * HD], lambda x: x + bias
            )

        row_max, row_total, summed = lax.fori_loop(
            0,
            n_seq,
            step,
            (
                jnp.full((rows, 1), neg_fill, jnp.float32),
                jnp.zeros((rows, 1), jnp.float32),
                jnp.zeros((rows, HD), jnp.float32),
            ),
        )
        m_s[h] = row_max
        l_s[h] = row_total
        acc_s[h] = summed
        return carry

    lax.fori_loop(0, heads, cached_head, 0)

    for k in range(1, chips):
        nx[k - 1].wait_recv()
        src = x_source(k)
        c = remote(newb.at[src], newb.at[src], ns_s.at[k], ns_r.at[k], sibling)
        c.start()
        ns.append(c)
    for c in ns:
        c.wait_recv()

    group = 4 if n_seq % 4 == 0 else 1
    span_keys = group * rows

    def new_head(h, carry):
        q = queries[h]

        def step(i, state):
            block = newb[pl.ds(i * group, group)].reshape(span_keys, 2 * HD)
            place = i * span_keys + lax.broadcasted_iota(jnp.int32, (rows, span_keys), 1)
            own = s * rows + lax.broadcasted_iota(jnp.int32, (rows, span_keys), 0)
            return update(
                state,
                q,
                block[:, 0:HD],
                block[:, HD : 2 * HD],
                lambda x: jnp.where(place <= own, x, neg_fill),
            )

        row_max, row_total, summed = lax.fori_loop(
            0, n_seq // group, step, (m_s[h], l_s[h], acc_s[h])
        )
        acc_s[h] = summed / row_total
        return carry

    lax.fori_loop(0, heads, new_head, 0)
    for h in range(heads):
        mixed[:, h * HD : (h + 1) * HD] = acc_s[h].astype(jnp.bfloat16)

    loads[2].wait()

    def share(owner):
        part = pl.ds(pl.multiple_of(owner * width, HD), width)
        return jnp.dot(mixed[...], wo[:, part], preferred_element_type=jnp.float32)

    order = list(range(1, NZ)) + [0]
    ry = {}
    for k in order:
        ysend[k] = share(lax.rem(z + k, NZ) * 2 + 1 - y).astype(jnp.bfloat16)
        ry[k] = remote(ysend.at[k], yrecv.at[k], ry_s.at[k], ry_r.at[k], y_peer)
        ry[k].start()

    rz = {}
    for k in range(1, NZ):
        own = share(lax.rem(z + k, NZ) * 2 + y)
        ry[k].wait_recv()
        zsend[k] = (own + yrecv[k].astype(jnp.float32)).astype(jnp.bfloat16)
        rz[k] = remote(zsend.at[k], zrecv.at[k], rz_s.at[k], rz_r.at[k], z_peer(k))
        rz[k].start()

    for k in range(1, chips):
        src = x_source(k)
        mx[k - 1].wait_recv()
        c = remote(map_all.at[src], map_all.at[src], ms_s.at[k], ms_r.at[k], sibling)
        c.start()
        ms.append(c)
        fx[k - 1].wait_recv()
        c = remote(fin_all.at[src], fin_all.at[src], fs_s.at[k], fs_r.at[k], sibling)
        c.start()
        fs.append(c)

    result = share(z * 2 + y)
    ry[0].wait_recv()
    result = result + yrecv[0].astype(jnp.float32)
    for k in range(1, NZ):
        rz[k].wait_recv()
        result = result + zrecv[k].astype(jnp.float32)
    att[...] = result.astype(jnp.bfloat16)

    for c in fs + ms:
        c.wait_recv()
    local_fin.wait()
    local_map.wait()
    for c in tz + ty + cx + cs + nx + ns + fx + fs + mx + ms + list(ry.values()) + list(rz.values()):
        c.wait_send()


def pool_kernel(n_seq, capacity, fin_all, map_all, out, zeros, sem):
    me = lax.axis_index("seq")
    zeros[...] = jnp.zeros_like(zeros)

    def place(source, carry):
        def inner(r, carry2):
            number = map_all[source, 0, me * capacity + r]
            target = out.at[:, pl.ds((source * capacity + r) * BLK, BLK)]

            @pl.when(number >= 0)
            def _():
                pltpu.make_async_copy(
                    fin_all.at[source, :, pl.ds(number * BLK, BLK)], target, sem
                ).start()

            @pl.when(number < 0)
            def _():
                pltpu.make_async_copy(zeros, target, sem).start()

            return carry2

        return lax.fori_loop(0, capacity, inner, carry)

    lax.fori_loop(0, n_seq, place, 0)
    pltpu.make_async_copy(out, out, sem).wait()


def on_device(
    n_seq, n_tp,
    tokens, norm_gain, q_weight, kv_weight, out_weight, ctx_cache, span_start,
    finished_cache, block_dest,
):
    rows, width = tokens.shape
    ctx_rows = ctx_cache.shape[0]
    heads = q_weight.shape[1] // HD
    chips = n_seq // 2
    seq_place = lax.axis_index("seq")
    positions = (span_start[0] + seq_place * rows + jnp.arange(rows, dtype=jnp.int32)).astype(
        jnp.float32
    )
    half = HD // 2
    frequency = jnp.exp(
        jnp.arange(half, dtype=jnp.float32) * (-2.0 * math.log(rope_base) / HD)
    )
    angles = positions[:, None] * frequency[None, :]
    cosine, sine = jnp.cos(angles), jnp.sin(angles)
    cosf = jnp.concatenate([cosine, cosine], 1)
    sinf = jnp.concatenate([-sine, sine], 1)
    blocks = block_dest.shape[0]
    capacity = 2 * blocks // n_seq
    slots = n_seq * capacity

    vmem = pl.BlockSpec(memory_space=pltpu.VMEM)
    anywhere = pl.BlockSpec(memory_space=pl.ANY)
    smem = pl.BlockSpec(memory_space=pltpu.SMEM)
    bf, f32 = jnp.bfloat16, jnp.float32
    dma = pltpu.SemaphoreType.DMA
    attended, fin_all, map_all = pl.pallas_call(
        functools.partial(layer_kernel, n_seq),
        out_shape=(
            jax.ShapeDtypeStruct((rows, width), bf),
            jax.ShapeDtypeStruct((n_seq,) + finished_cache.shape, bf),
            jax.ShapeDtypeStruct((n_seq, 8, slots), jnp.int32),
        ),
        in_specs=[
            vmem, vmem, anywhere, anywhere, anywhere, anywhere, vmem, vmem, smem, anywhere,
            vmem, vmem,
        ],
        out_specs=(vmem, anywhere, anywhere),
        scratch_shapes=[
            pltpu.VMEM((n_tp, rows, width), bf),
            pltpu.VMEM(q_weight.shape, bf),
            pltpu.VMEM((D, 2 * HD), bf),
            pltpu.VMEM(out_weight.shape, bf),
            pltpu.VMEM((n_seq, ctx_rows, 2 * HD), bf),
            pltpu.VMEM((n_seq, rows, 2 * HD), bf),
            pltpu.VMEM((8, slots), jnp.int32),
            pltpu.VMEM((rows, width), f32),
            pltpu.VMEM((rows, 2 * HD), f32),
            pltpu.VMEM((heads, rows, HD), bf),
            pltpu.VMEM((heads, rows, 1), f32),
            pltpu.VMEM((heads, rows, 1), f32),
            pltpu.VMEM((heads, rows, HD), f32),
            pltpu.VMEM((rows, width), bf),
            pltpu.VMEM((NZ, rows, width), bf),
            pltpu.VMEM((NZ, rows, width), bf),
            pltpu.VMEM((NZ, rows, width), bf),
            pltpu.VMEM((NZ, rows, width), bf),
            dma((3,)),
            dma((3,)),
        ]
        + [dma((NZ,))] * 4
        + [dma((chips,))] * 16
        + [dma((NZ,))] * 4,
        compiler_params=pltpu.CompilerParams(
            collective_id=0, has_side_effects=True, vmem_limit_bytes=56 * 1024 * 1024
        ),
        name="layer",
    )(
        tokens,
        norm_gain.reshape(n_tp, 1, width),
        q_weight,
        kv_weight.reshape(D, 2 * HD),
        out_weight,
        ctx_cache.reshape(ctx_rows, 2 * HD),
        cosf,
        sinf,
        span_start,
        finished_cache,
        block_dest,
        block_dest.reshape(1, blocks),
    )
    page_pool = pl.pallas_call(
        functools.partial(pool_kernel, n_seq, capacity),
        out_shape=jax.ShapeDtypeStruct(
            (LAYERS, slots * BLK) + finished_cache.shape[2:], bf
        ),
        in_specs=[anywhere, smem],
        out_specs=anywhere,
        scratch_shapes=[
            pltpu.VMEM((LAYERS, BLK) + finished_cache.shape[2:], bf),
            dma,
        ],
        name="pool",
    )(fin_all, map_all)
    return (attended, page_pool)


def solution(mesh):
    return jax.shard_map(
        functools.partial(on_device, mesh.shape["seq"], mesh.shape["tp"]),
        mesh=mesh,
        in_specs=(
            P("seq", "tp"),
            P(),
            P(None, "tp"),
            P(None, None, "tp"),
            P("tp", None),
            P("seq", None, "tp"),
            P(),
            P(None, "seq", None, "tp"),
            P("seq", None),
        ),
        out_specs=(P("seq", "tp"), P(None, "seq", None, "tp")),
        check_vma=False,
    )
```

```python
import functools
import math

import jax
import jax.numpy as jnp
from jax import lax
from jax.experimental import pallas as pl
from jax.experimental.pallas import tpu as pltpu
from jax.sharding import PartitionSpec as P

D = 5120
HD = 128
LAYERS = 4
BLK = 16
NZ = 4

rms_eps = 1e-06
rope_base = 1000000.0
neg_fill = -1e30
MESH = pl.DeviceIdType.MESH


def layer_kernel(
    n_seq, in_vmem, tokens, gain, qw, kvw, ow, ctx, cosf, sinf, span, fin, bdc, bdr,
    att, fin_all, map_all,
    tok, wq, wkv, wo, ctxb, newb, mapb, qacc, kvacc, queries, m_s, l_s, acc_s, mixed,
    ysend, yrecv, zsend, zrecv, fin_buf,
    wsem, lsem, tz_s, tz_r, ty_s, ty_r, cx_s, cx_r, cs_s, cs_r, nx_s, nx_r, ns_s, ns_r,
    fx_s, fx_r, fs_s, fs_r, mx_s, mx_r, ms_s, ms_r, ry_s, ry_r, rz_s, rz_r, fin_d,
):
    s = lax.axis_index("seq")
    t = lax.axis_index("tp")
    z, y = t // 2, t % 2
    chip, core = s // 2, s % 2
    chips = n_seq // 2
    rows, width = tokens.shape
    heads = width // HD
    ctx_rows = ctx.shape[0]

    def z_peer(k):
        return {"tp": lax.rem(z + k, NZ) * 2 + y}

    y_peer = {"tp": z * 2 + 1 - y}
    sibling = {"seq": chip * 2 + 1 - core}

    def x_peer(k):
        return {"seq": lax.rem(chip + k, chips) * 2 + core}

    def x_source(k):
        return lax.rem(chip + chips - k, chips) * 2 + core

    def remote(src, dst, ssem, rsem, device):
        return pltpu.make_async_remote_copy(
            src_ref=src, dst_ref=dst, send_sem=ssem, recv_sem=rsem,
            device_id=device, device_id_type=MESH,
        )

    held = fin_buf if in_vmem else fin_all
    local_fin = pltpu.make_async_copy(fin, held.at[s], lsem.at[1])
    local_fin.start()

    loads = [
        pltpu.make_async_copy(qw, wq, wsem.at[0]),
        pltpu.make_async_copy(kvw, wkv, wsem.at[1]),
        pltpu.make_async_copy(ow, wo, wsem.at[2]),
    ]

    barrier = pltpu.get_barrier_semaphore()
    peers = [z_peer(k) for k in range(1, NZ)] + [y_peer, sibling]
    peers += [x_peer(k) for k in range(1, chips)]
    for peer in peers:
        pl.semaphore_signal(barrier, inc=1, device_id=peer, device_id_type=MESH)
    pl.semaphore_wait(barrier, len(peers))

    tz = [
        remote(tokens, tok.at[k], tz_s.at[k], tz_r.at[k], z_peer(k)) for k in range(1, NZ)
    ]
    ty = [remote(tokens, tok.at[NZ], ty_s.at[0], ty_r.at[0], y_peer)]
    ty[0].start()
    for c in tz:
        c.start()

    cx = [
        remote(ctx, ctxb.at[s], cx_s.at[k], cx_r.at[k], x_peer(k)) for k in range(1, chips)
    ]
    for c in cx:
        c.start()
    cs = [remote(ctx, ctxb.at[s], cs_s.at[0], cs_r.at[0], sibling)]
    cs[0].start()
    for w in loads:
        w.start()
    local_ctx = pltpu.make_async_copy(ctx, ctxb.at[s], lsem.at[0])
    local_ctx.start()

    local_fin.wait()
    fx = [
        remote(held.at[s], held.at[s], fx_s.at[k], fx_r.at[k], x_peer(k))
        for k in range(1, chips)
    ]
    for c in fx:
        c.start()
    fs = [remote(held.at[s], held.at[s], fs_s.at[0], fs_r.at[0], sibling)]
    fs[0].start()
    drains = []

    def drain(src):
        if in_vmem:
            c = pltpu.make_async_copy(held.at[src], fin_all.at[src], fin_d.at[len(drains)])
            c.start()
            drains.append(c)

    drain(s)

    blocks = bdc.shape[0]
    capacity = 2 * blocks // n_seq
    slots = n_seq * capacity
    earlier = (
        lax.broadcasted_iota(jnp.int32, (blocks, blocks), 1)
        < lax.broadcasted_iota(jnp.int32, (blocks, blocks), 0)
    )
    same = bdr[...] == bdc[...]
    rank = jnp.sum(jnp.where(earlier & same, 1.0, 0.0), axis=1, keepdims=True).astype(jnp.int32)
    slot = bdc[...] * capacity + rank
    match = slot == lax.broadcasted_iota(jnp.int32, (blocks, slots), 1)
    numbers = lax.broadcasted_iota(jnp.int32, (blocks, slots), 0).astype(jnp.float32) + 1.0
    source = jnp.sum(jnp.where(match, numbers, 0.0), axis=0, keepdims=True).astype(jnp.int32) - 1
    mapb[...] = jnp.broadcast_to(source, mapb.shape)
    mx = [
        remote(mapb, map_all.at[s], mx_s.at[k], mx_r.at[k], x_peer(k)) for k in range(1, chips)
    ]
    for c in mx:
        c.start()
    ms = [remote(mapb, map_all.at[s], ms_s.at[0], ms_r.at[0], sibling)]
    ms[0].start()
    local_map = pltpu.make_async_copy(mapb, map_all.at[s], lsem.at[2])
    local_map.start()

    tok[0] = tokens[...]

    for k in range(1, NZ):
        tz[k - 1].wait_recv()
        c = remote(tok.at[k], tok.at[NZ + k], ty_s.at[k], ty_r.at[k], y_peer)
        c.start()
        ty.append(c)
    for k in range(1, chips):
        cx[k - 1].wait_recv()
        src = x_source(k)
        c = remote(ctxb.at[src], ctxb.at[src], cs_s.at[k], cs_r.at[k], sibling)
        c.start()
        cs.append(c)
    for c in ty:
        c.wait_recv()

    def squares(k, total):
        x = tok[k].astype(jnp.float32)
        return total + jnp.sum(x * x, axis=1, keepdims=True)

    total = lax.fori_loop(0, 2 * NZ, squares, jnp.zeros((rows, 1), jnp.float32))
    scale = lax.rsqrt(total / D + rms_eps)
    qacc[...] = jnp.zeros_like(qacc)
    kvacc[...] = jnp.zeros_like(kvacc)
    loads[0].wait()
    loads[1].wait()

    def project(k, carry):
        owner = lax.rem(z + NZ - lax.rem(k, NZ), NZ) * 2 + lax.rem(y + k // NZ, 2)
        x = tok[k].astype(jnp.float32)
        normed = (x * scale * gain[owner]).astype(jnp.bfloat16)
        part = pl.ds(pl.multiple_of(owner * width, HD), width)
        kvacc[...] += jnp.dot(normed, wkv[part, :], preferred_element_type=jnp.float32)
        qacc[...] += jnp.dot(normed, wq[part, :], preferred_element_type=jnp.float32)
        return carry

    lax.fori_loop(0, 2 * NZ, project, 0)
    cosine, sine = cosf[...], sinf[...]

    def rotate(x):
        return (x * cosine + pltpu.roll(x, HD // 2, 1) * sine).astype(jnp.bfloat16)

    newb[s, :, 0:HD] = rotate(kvacc[:, 0:HD])
    newb[s, :, HD : 2 * HD] = kvacc[:, HD : 2 * HD].astype(jnp.bfloat16)
    nx = [
        remote(newb.at[s], newb.at[s], nx_s.at[k], nx_r.at[k], x_peer(k)) for k in range(1, chips)
    ]
    for c in nx:
        c.start()
    ns = [remote(newb.at[s], newb.at[s], ns_s.at[0], ns_r.at[0], sibling)]
    ns[0].start()
    for h in range(heads):
        queries[h] = rotate(qacc[:, h * HD : (h + 1) * HD])

    local_ctx.wait()
    for c in cs:
        c.wait_recv()

    factor = HD**-0.5 * math.log2(math.e)
    span_first = span[0]

    def update(state, q, keys, values, mask):
        row_max, row_total, summed = state
        scores = mask(
            lax.dot_general(
                q, keys, (((1,), (1,)), ((), ())), preferred_element_type=jnp.float32
            )
            * factor
        )
        new_max = jnp.maximum(row_max, jnp.max(scores, axis=1, keepdims=True))
        weights = jnp.exp2(scores - new_max)
        rescale = jnp.exp2(row_max - new_max)
        return (
            new_max,
            row_total * rescale + jnp.sum(weights, axis=1, keepdims=True),
            summed * rescale
            + jnp.dot(
                weights.astype(jnp.bfloat16), values, preferred_element_type=jnp.float32
            ),
        )

    def cached_head(h, carry):
        q = queries[h]

        def step(i, state):
            place = i * ctx_rows + lax.broadcasted_iota(jnp.int32, (1, ctx_rows), 1)
            bias = jnp.where(place < span_first, 0.0, neg_fill)
            return update(
                state, q, ctxb[i, :, 0:HD], ctxb[i, :, HD : 2 * HD], lambda x: x + bias
            )

        row_max, row_total, summed = lax.fori_loop(
            0,
            n_seq,
            step,
            (
                jnp.full((rows, 1), neg_fill, jnp.float32),
                jnp.zeros((rows, 1), jnp.float32),
                jnp.zeros((rows, HD), jnp.float32),
            ),
        )
        m_s[h] = row_max
        l_s[h] = row_total
        acc_s[h] = summed
        return carry

    lax.fori_loop(0, heads, cached_head, 0)

    for k in range(1, chips):
        nx[k - 1].wait_recv()
        src = x_source(k)
        c = remote(newb.at[src], newb.at[src], ns_s.at[k], ns_r.at[k], sibling)
        c.start()
        ns.append(c)
    for c in ns:
        c.wait_recv()

    group = 4 if n_seq % 4 == 0 else 1
    span_keys = group * rows

    def new_head(h, carry):
        q = queries[h]

        def step(i, state):
            block = newb[pl.ds(i * group, group)].reshape(span_keys, 2 * HD)
            place = i * span_keys + lax.broadcasted_iota(jnp.int32, (rows, span_keys), 1)
            own = s * rows + lax.broadcasted_iota(jnp.int32, (rows, span_keys), 0)
            return update(
                state,
                q,
                block[:, 0:HD],
                block[:, HD : 2 * HD],
                lambda x: jnp.where(place <= own, x, neg_fill),
            )

        row_max, row_total, summed = lax.fori_loop(
            0, n_seq // group, step, (m_s[h], l_s[h], acc_s[h])
        )
        acc_s[h] = summed / row_total
        return carry

    lax.fori_loop(0, heads, new_head, 0)
    for h in range(heads):
        mixed[:, h * HD : (h + 1) * HD] = acc_s[h].astype(jnp.bfloat16)

    loads[2].wait()

    def share(owner):
        part = pl.ds(pl.multiple_of(owner * width, HD), width)
        return jnp.dot(mixed[...], wo[:, part], preferred_element_type=jnp.float32)

    order = list(range(1, NZ)) + [0]
    ry = {}
    for k in order:
        ysend[k] = share(lax.rem(z + k, NZ) * 2 + 1 - y).astype(jnp.bfloat16)
        ry[k] = remote(ysend.at[k], yrecv.at[k], ry_s.at[k], ry_r.at[k], y_peer)
        ry[k].start()

    rz = {}
    for k in range(1, NZ):
        own = share(lax.rem(z + k, NZ) * 2 + y)
        ry[k].wait_recv()
        zsend[k] = (own + yrecv[k].astype(jnp.float32)).astype(jnp.bfloat16)
        rz[k] = remote(zsend.at[k], zrecv.at[k], rz_s.at[k], rz_r.at[k], z_peer(k))
        rz[k].start()

    for k in range(1, chips):
        src = x_source(k)
        mx[k - 1].wait_recv()
        c = remote(map_all.at[src], map_all.at[src], ms_s.at[k], ms_r.at[k], sibling)
        c.start()
        ms.append(c)
        fx[k - 1].wait_recv()
        c = remote(held.at[src], held.at[src], fs_s.at[k], fs_r.at[k], sibling)
        c.start()
        fs.append(c)
        drain(src)

    result = share(z * 2 + y)
    ry[0].wait_recv()
    result = result + yrecv[0].astype(jnp.float32)
    for k in range(1, NZ):
        rz[k].wait_recv()
        result = result + zrecv[k].astype(jnp.float32)
    att[...] = result.astype(jnp.bfloat16)

    for c in ms:
        c.wait_recv()
    for k in range(chips):
        fs[k].wait_recv()
        drain(lax.rem(chip + chips - k, chips) * 2 + 1 - core)
    for c in drains:
        c.wait()
    local_map.wait()
    for c in tz + ty + cx + cs + nx + ns + fx + fs + mx + ms + list(ry.values()) + list(rz.values()):
        c.wait_send()


def pool_kernel(n_seq, capacity, fin_all, map_all, out, zeros, held, sem, in_sem):
    me = lax.axis_index("seq")
    for source in range(n_seq):
        pltpu.make_async_copy(fin_all.at[source], held.at[source], in_sem.at[source]).start()
    zeros[...] = jnp.zeros_like(zeros)

    def place(source, carry):
        pltpu.make_async_copy(fin_all.at[source], held.at[source], in_sem.at[source]).wait()

        def inner(r, carry2):
            number = map_all[source, 0, me * capacity + r]
            target = out.at[:, pl.ds((source * capacity + r) * BLK, BLK)]

            @pl.when(number >= 0)
            def _():
                pltpu.make_async_copy(
                    held.at[source, :, pl.ds(number * BLK, BLK)], target, sem
                ).start()

            @pl.when(number < 0)
            def _():
                pltpu.make_async_copy(zeros, target, sem).start()

            return carry2

        return lax.fori_loop(0, capacity, inner, carry)

    lax.fori_loop(0, n_seq, place, 0)
    pltpu.make_async_copy(out, out, sem).wait()


def on_device(
    n_seq, n_tp,
    tokens, norm_gain, q_weight, kv_weight, out_weight, ctx_cache, span_start,
    finished_cache, block_dest,
):
    rows, width = tokens.shape
    ctx_rows = ctx_cache.shape[0]
    heads = q_weight.shape[1] // HD
    chips = n_seq // 2
    seq_place = lax.axis_index("seq")
    positions = (span_start[0] + seq_place * rows + jnp.arange(rows, dtype=jnp.int32)).astype(
        jnp.float32
    )
    half = HD // 2
    frequency = jnp.exp(
        jnp.arange(half, dtype=jnp.float32) * (-2.0 * math.log(rope_base) / HD)
    )
    angles = positions[:, None] * frequency[None, :]
    cosine, sine = jnp.cos(angles), jnp.sin(angles)
    cosf = jnp.concatenate([cosine, cosine], 1)
    sinf = jnp.concatenate([-sine, sine], 1)
    blocks = block_dest.shape[0]
    capacity = 2 * blocks // n_seq
    slots = n_seq * capacity

    in_vmem = n_seq * finished_cache.size * 2 <= 12 * 1024 * 1024
    vmem = pl.BlockSpec(memory_space=pltpu.VMEM)
    anywhere = pl.BlockSpec(memory_space=pl.ANY)
    smem = pl.BlockSpec(memory_space=pltpu.SMEM)
    bf, f32 = jnp.bfloat16, jnp.float32
    dma = pltpu.SemaphoreType.DMA
    attended, fin_all, map_all = pl.pallas_call(
        functools.partial(layer_kernel, n_seq, in_vmem),
        out_shape=(
            jax.ShapeDtypeStruct((rows, width), bf),
            jax.ShapeDtypeStruct((n_seq,) + finished_cache.shape, bf),
            jax.ShapeDtypeStruct((n_seq, 8, slots), jnp.int32),
        ),
        in_specs=[
            vmem, vmem, anywhere, anywhere, anywhere, anywhere, vmem, vmem, smem, anywhere,
            vmem, vmem,
        ],
        out_specs=(vmem, anywhere, anywhere),
        scratch_shapes=[
            pltpu.VMEM((n_tp, rows, width), bf),
            pltpu.VMEM(q_weight.shape, bf),
            pltpu.VMEM((D, 2 * HD), bf),
            pltpu.VMEM(out_weight.shape, bf),
            pltpu.VMEM((n_seq, ctx_rows, 2 * HD), bf),
            pltpu.VMEM((n_seq, rows, 2 * HD), bf),
            pltpu.VMEM((8, slots), jnp.int32),
            pltpu.VMEM((rows, width), f32),
            pltpu.VMEM((rows, 2 * HD), f32),
            pltpu.VMEM((heads, rows, HD), bf),
            pltpu.VMEM((heads, rows, 1), f32),
            pltpu.VMEM((heads, rows, 1), f32),
            pltpu.VMEM((heads, rows, HD), f32),
            pltpu.VMEM((rows, width), bf),
            pltpu.VMEM((NZ, rows, width), bf),
            pltpu.VMEM((NZ, rows, width), bf),
            pltpu.VMEM((NZ, rows, width), bf),
            pltpu.VMEM((NZ, rows, width), bf),
            pltpu.VMEM(((n_seq,) + finished_cache.shape) if in_vmem else (8, HD), bf),
            dma((3,)),
            dma((3,)),
        ]
        + [dma((NZ,))] * 4
        + [dma((chips,))] * 16
        + [dma((NZ,))] * 4
        + [dma((n_seq,))],
        compiler_params=pltpu.CompilerParams(
            collective_id=0, has_side_effects=True, vmem_limit_bytes=56 * 1024 * 1024
        ),
        name="layer",
    )(
        tokens,
        norm_gain.reshape(n_tp, 1, width),
        q_weight,
        kv_weight.reshape(D, 2 * HD),
        out_weight,
        ctx_cache.reshape(ctx_rows, 2 * HD),
        cosf,
        sinf,
        span_start,
        finished_cache,
        block_dest,
        block_dest.reshape(1, blocks),
    )
    page_pool = pl.pallas_call(
        functools.partial(pool_kernel, n_seq, capacity),
        out_shape=jax.ShapeDtypeStruct(
            (LAYERS, slots * BLK) + finished_cache.shape[2:], bf
        ),
        in_specs=[anywhere, smem],
        out_specs=anywhere,
        scratch_shapes=[
            pltpu.VMEM((LAYERS, BLK) + finished_cache.shape[2:], bf),
            pltpu.VMEM((n_seq,) + finished_cache.shape, bf),
            dma,
            dma((n_seq,)),
        ],
        compiler_params=pltpu.CompilerParams(vmem_limit_bytes=56 * 1024 * 1024),
        name="pool",
    )(fin_all, map_all)
    return (attended, page_pool)


def solution(mesh):
    return jax.shard_map(
        functools.partial(on_device, mesh.shape["seq"], mesh.shape["tp"]),
        mesh=mesh,
        in_specs=(
            P("seq", "tp"),
            P(),
            P(None, "tp"),
            P(None, None, "tp"),
            P("tp", None),
            P("seq", None, "tp"),
            P(),
            P(None, "seq", None, "tp"),
            P("seq", None),
        ),
        out_specs=(P("seq", "tp"), P(None, "seq", None, "tp")),
        check_vma=False,
    )
```

```python
import functools
import math

import jax
import jax.numpy as jnp
from jax import lax
from jax.experimental import pallas as pl
from jax.experimental.pallas import tpu as pltpu
from jax.sharding import PartitionSpec as P

D = 5120
HD = 128
LAYERS = 4
BLK = 16
NZ = 4

rms_eps = 1e-06
rope_base = 1000000.0
neg_fill = -1e30
MESH = pl.DeviceIdType.MESH


def layer_kernel(
    n_seq, in_vmem, tokens, gain, qw, kvw, ow, ctx, cosf, sinf, span, fin, bdc, bdr,
    att, fin_all, map_all,
    tok, wq, wkv, wo, ctxb, newb, mapb, qacc, kvacc, queries, m_s, l_s, acc_s, mixed,
    ysend, yrecv, zsend, zrecv, fin_buf,
    wsem, lsem, tz_s, tz_r, ty_s, ty_r, cx_s, cx_r, cs_s, cs_r, nx_s, nx_r, ns_s, ns_r,
    fx_s, fx_r, fs_s, fs_r, mx_s, mx_r, ms_s, ms_r, ry_s, ry_r, rz_s, rz_r, fin_d,
):
    s = lax.axis_index("seq")
    t = lax.axis_index("tp")
    z, y = t // 2, t % 2
    chip, core = s // 2, s % 2
    chips = n_seq // 2
    rows, width = tokens.shape
    heads = width // HD
    ctx_rows = ctx.shape[0]

    def z_peer(k):
        return {"tp": lax.rem(z + k, NZ) * 2 + y}

    y_peer = {"tp": z * 2 + 1 - y}
    sibling = {"seq": chip * 2 + 1 - core}

    def x_peer(k):
        return {"seq": lax.rem(chip + k, chips) * 2 + core}

    def x_source(k):
        return lax.rem(chip + chips - k, chips) * 2 + core

    def remote(src, dst, ssem, rsem, device):
        return pltpu.make_async_remote_copy(
            src_ref=src, dst_ref=dst, send_sem=ssem, recv_sem=rsem,
            device_id=device, device_id_type=MESH,
        )

    held = fin_buf if in_vmem else fin_all
    local_fin = pltpu.make_async_copy(fin, held.at[s], lsem.at[1])
    local_fin.start()

    loads = [
        pltpu.make_async_copy(qw, wq, wsem.at[0]),
        pltpu.make_async_copy(kvw, wkv, wsem.at[1]),
        pltpu.make_async_copy(ow, wo, wsem.at[2]),
    ]

    barrier = pltpu.get_barrier_semaphore()
    peers = [z_peer(k) for k in range(1, NZ)] + [y_peer, sibling]
    peers += [x_peer(k) for k in range(1, chips)]
    for peer in peers:
        pl.semaphore_signal(barrier, inc=1, device_id=peer, device_id_type=MESH)
    pl.semaphore_wait(barrier, len(peers))

    tz = [
        remote(tokens, tok.at[k], tz_s.at[k], tz_r.at[k], z_peer(k)) for k in range(1, NZ)
    ]
    ty = [remote(tokens, tok.at[NZ], ty_s.at[0], ty_r.at[0], y_peer)]
    ty[0].start()
    for c in tz:
        c.start()

    cx = [
        remote(ctx, ctxb.at[s], cx_s.at[k], cx_r.at[k], x_peer(k)) for k in range(1, chips)
    ]
    for c in cx:
        c.start()
    cs = [remote(ctx, ctxb.at[s], cs_s.at[0], cs_r.at[0], sibling)]
    cs[0].start()
    for w in loads:
        w.start()
    local_ctx = pltpu.make_async_copy(ctx, ctxb.at[s], lsem.at[0])
    local_ctx.start()

    local_fin.wait()
    fx = [
        remote(held.at[s], held.at[s], fx_s.at[k], fx_r.at[k], x_peer(k))
        for k in range(1, chips)
    ]
    for c in fx:
        c.start()
    fs = [remote(held.at[s], held.at[s], fs_s.at[0], fs_r.at[0], sibling)]
    fs[0].start()
    drains = []

    def drain(src):
        if in_vmem:
            c = pltpu.make_async_copy(held.at[src], fin_all.at[src], fin_d.at[len(drains)])
            c.start()
            drains.append(c)

    drain(s)

    blocks = bdc.shape[0]
    capacity = 2 * blocks // n_seq
    slots = n_seq * capacity
    earlier = (
        lax.broadcasted_iota(jnp.int32, (blocks, blocks), 1)
        < lax.broadcasted_iota(jnp.int32, (blocks, blocks), 0)
    )
    same = bdr[...] == bdc[...]
    rank = jnp.sum(jnp.where(earlier & same, 1.0, 0.0), axis=1, keepdims=True).astype(jnp.int32)
    slot = bdc[...] * capacity + rank
    match = slot == lax.broadcasted_iota(jnp.int32, (blocks, slots), 1)
    numbers = lax.broadcasted_iota(jnp.int32, (blocks, slots), 0).astype(jnp.float32) + 1.0
    source = jnp.sum(jnp.where(match, numbers, 0.0), axis=0, keepdims=True).astype(jnp.int32) - 1
    mapb[...] = jnp.broadcast_to(source, mapb.shape)
    mx = [
        remote(mapb, map_all.at[s], mx_s.at[k], mx_r.at[k], x_peer(k)) for k in range(1, chips)
    ]
    for c in mx:
        c.start()
    ms = [remote(mapb, map_all.at[s], ms_s.at[0], ms_r.at[0], sibling)]
    ms[0].start()
    local_map = pltpu.make_async_copy(mapb, map_all.at[s], lsem.at[2])
    local_map.start()

    tok[0] = tokens[...]

    for k in range(1, NZ):
        tz[k - 1].wait_recv()
        c = remote(tok.at[k], tok.at[NZ + k], ty_s.at[k], ty_r.at[k], y_peer)
        c.start()
        ty.append(c)
    for k in range(1, chips):
        cx[k - 1].wait_recv()
        src = x_source(k)
        c = remote(ctxb.at[src], ctxb.at[src], cs_s.at[k], cs_r.at[k], sibling)
        c.start()
        cs.append(c)
    for c in ty:
        c.wait_recv()

    def squares(k, total):
        x = tok[k].astype(jnp.float32)
        return total + jnp.sum(x * x, axis=1, keepdims=True)

    total = lax.fori_loop(0, 2 * NZ, squares, jnp.zeros((rows, 1), jnp.float32))
    scale = lax.rsqrt(total / D + rms_eps)
    qacc[...] = jnp.zeros_like(qacc)
    kvacc[...] = jnp.zeros_like(kvacc)
    loads[0].wait()
    loads[1].wait()

    def project(k, carry):
        owner = lax.rem(z + NZ - lax.rem(k, NZ), NZ) * 2 + lax.rem(y + k // NZ, 2)
        x = tok[k].astype(jnp.float32)
        normed = (x * scale * gain[owner]).astype(jnp.bfloat16)
        part = pl.ds(pl.multiple_of(owner * width, HD), width)
        kvacc[...] += jnp.dot(normed, wkv[part, :], preferred_element_type=jnp.float32)
        qacc[...] += jnp.dot(normed, wq[part, :], preferred_element_type=jnp.float32)
        return carry

    lax.fori_loop(0, 2 * NZ, project, 0)
    cosine, sine = cosf[...], sinf[...]

    def rotate(x):
        return (x * cosine + pltpu.roll(x, HD // 2, 1) * sine).astype(jnp.bfloat16)

    newb[s, :, 0:HD] = rotate(kvacc[:, 0:HD])
    newb[s, :, HD : 2 * HD] = kvacc[:, HD : 2 * HD].astype(jnp.bfloat16)
    nx = [
        remote(newb.at[s], newb.at[s], nx_s.at[k], nx_r.at[k], x_peer(k)) for k in range(1, chips)
    ]
    for c in nx:
        c.start()
    ns = [remote(newb.at[s], newb.at[s], ns_s.at[0], ns_r.at[0], sibling)]
    ns[0].start()
    for h in range(heads):
        queries[h] = rotate(qacc[:, h * HD : (h + 1) * HD])

    local_ctx.wait()
    for c in cs:
        c.wait_recv()

    factor = HD**-0.5 * math.log2(math.e)
    span_first = span[0]

    def update(state, q, keys, values, mask):
        row_max, row_total, summed = state
        scores = mask(
            lax.dot_general(
                q, keys, (((1,), (1,)), ((), ())), preferred_element_type=jnp.float32
            )
            * factor
        )
        new_max = jnp.maximum(row_max, jnp.max(scores, axis=1, keepdims=True))
        weights = jnp.exp2(scores - new_max)
        rescale = jnp.exp2(row_max - new_max)
        return (
            new_max,
            row_total * rescale + jnp.sum(weights, axis=1, keepdims=True),
            summed * rescale
            + jnp.dot(
                weights.astype(jnp.bfloat16), values, preferred_element_type=jnp.float32
            ),
        )

    def cached_head(h, carry):
        q = queries[h]

        def step(i, state):
            place = i * ctx_rows + lax.broadcasted_iota(jnp.int32, (1, ctx_rows), 1)
            bias = jnp.where(place < span_first, 0.0, neg_fill)
            return update(
                state, q, ctxb[i, :, 0:HD], ctxb[i, :, HD : 2 * HD], lambda x: x + bias
            )

        row_max, row_total, summed = lax.fori_loop(
            0,
            n_seq,
            step,
            (
                jnp.full((rows, 1), neg_fill, jnp.float32),
                jnp.zeros((rows, 1), jnp.float32),
                jnp.zeros((rows, HD), jnp.float32),
            ),
            unroll=n_seq <= 4,
        )
        m_s[h] = row_max
        l_s[h] = row_total
        acc_s[h] = summed
        return carry

    lax.fori_loop(0, heads, cached_head, 0)

    for k in range(1, chips):
        nx[k - 1].wait_recv()
        src = x_source(k)
        c = remote(newb.at[src], newb.at[src], ns_s.at[k], ns_r.at[k], sibling)
        c.start()
        ns.append(c)
    for c in ns:
        c.wait_recv()

    group = 4 if n_seq % 4 == 0 else 1
    span_keys = group * rows

    def new_head(h, carry):
        q = queries[h]

        def step(i, state):
            block = newb[pl.ds(i * group, group)].reshape(span_keys, 2 * HD)
            place = i * span_keys + lax.broadcasted_iota(jnp.int32, (rows, span_keys), 1)
            own = s * rows + lax.broadcasted_iota(jnp.int32, (rows, span_keys), 0)
            return update(
                state,
                q,
                block[:, 0:HD],
                block[:, HD : 2 * HD],
                lambda x: jnp.where(place <= own, x, neg_fill),
            )

        row_max, row_total, summed = lax.fori_loop(
            0, n_seq // group, step, (m_s[h], l_s[h], acc_s[h])
        )
        acc_s[h] = summed / row_total
        return carry

    lax.fori_loop(0, heads, new_head, 0)
    for h in range(heads):
        mixed[:, h * HD : (h + 1) * HD] = acc_s[h].astype(jnp.bfloat16)

    loads[2].wait()

    def share(owner):
        part = pl.ds(pl.multiple_of(owner * width, HD), width)
        return jnp.dot(mixed[...], wo[:, part], preferred_element_type=jnp.float32)

    order = list(range(1, NZ)) + [0]
    ry = {}
    for k in order:
        ysend[k] = share(lax.rem(z + k, NZ) * 2 + 1 - y).astype(jnp.bfloat16)
        ry[k] = remote(ysend.at[k], yrecv.at[k], ry_s.at[k], ry_r.at[k], y_peer)
        ry[k].start()

    rz = {}
    for k in range(1, NZ):
        own = share(lax.rem(z + k, NZ) * 2 + y)
        ry[k].wait_recv()
        zsend[k] = (own + yrecv[k].astype(jnp.float32)).astype(jnp.bfloat16)
        rz[k] = remote(zsend.at[k], zrecv.at[k], rz_s.at[k], rz_r.at[k], z_peer(k))
        rz[k].start()

    for k in range(1, chips):
        src = x_source(k)
        mx[k - 1].wait_recv()
        c = remote(map_all.at[src], map_all.at[src], ms_s.at[k], ms_r.at[k], sibling)
        c.start()
        ms.append(c)
        fx[k - 1].wait_recv()
        c = remote(held.at[src], held.at[src], fs_s.at[k], fs_r.at[k], sibling)
        c.start()
        fs.append(c)
        drain(src)

    result = share(z * 2 + y)
    ry[0].wait_recv()
    result = result + yrecv[0].astype(jnp.float32)
    for k in range(1, NZ):
        rz[k].wait_recv()
        result = result + zrecv[k].astype(jnp.float32)
    att[...] = result.astype(jnp.bfloat16)

    for c in ms:
        c.wait_recv()
    for k in range(chips):
        fs[k].wait_recv()
        drain(lax.rem(chip + chips - k, chips) * 2 + 1 - core)
    for c in drains:
        c.wait()
    local_map.wait()
    for c in tz + ty + cx + cs + nx + ns + fx + fs + mx + ms + list(ry.values()) + list(rz.values()):
        c.wait_send()


def pool_kernel(n_seq, capacity, fin_all, map_all, out, zeros, held, sem, in_sem):
    me = lax.axis_index("seq")
    for source in range(n_seq):
        pltpu.make_async_copy(fin_all.at[source], held.at[source], in_sem.at[source]).start()
    zeros[...] = jnp.zeros_like(zeros)

    def place(source, carry):
        pltpu.make_async_copy(fin_all.at[source], held.at[source], in_sem.at[source]).wait()

        def inner(r, carry2):
            number = map_all[source, 0, me * capacity + r]
            target = out.at[:, pl.ds((source * capacity + r) * BLK, BLK)]

            @pl.when(number >= 0)
            def _():
                pltpu.make_async_copy(
                    held.at[source, :, pl.ds(number * BLK, BLK)], target, sem
                ).start()

            @pl.when(number < 0)
            def _():
                pltpu.make_async_copy(zeros, target, sem).start()

            return carry2

        return lax.fori_loop(0, capacity, inner, carry)

    lax.fori_loop(0, n_seq, place, 0)
    pltpu.make_async_copy(out, out, sem).wait()


def on_device(
    n_seq, n_tp,
    tokens, norm_gain, q_weight, kv_weight, out_weight, ctx_cache, span_start,
    finished_cache, block_dest,
):
    rows, width = tokens.shape
    ctx_rows = ctx_cache.shape[0]
    heads = q_weight.shape[1] // HD
    chips = n_seq // 2
    seq_place = lax.axis_index("seq")
    positions = (span_start[0] + seq_place * rows + jnp.arange(rows, dtype=jnp.int32)).astype(
        jnp.float32
    )
    half = HD // 2
    frequency = jnp.exp(
        jnp.arange(half, dtype=jnp.float32) * (-2.0 * math.log(rope_base) / HD)
    )
    angles = positions[:, None] * frequency[None, :]
    cosine, sine = jnp.cos(angles), jnp.sin(angles)
    cosf = jnp.concatenate([cosine, cosine], 1)
    sinf = jnp.concatenate([-sine, sine], 1)
    blocks = block_dest.shape[0]
    capacity = 2 * blocks // n_seq
    slots = n_seq * capacity

    in_vmem = n_seq * finished_cache.size * 2 <= 12 * 1024 * 1024
    vmem = pl.BlockSpec(memory_space=pltpu.VMEM)
    anywhere = pl.BlockSpec(memory_space=pl.ANY)
    smem = pl.BlockSpec(memory_space=pltpu.SMEM)
    bf, f32 = jnp.bfloat16, jnp.float32
    dma = pltpu.SemaphoreType.DMA
    attended, fin_all, map_all = pl.pallas_call(
        functools.partial(layer_kernel, n_seq, in_vmem),
        out_shape=(
            jax.ShapeDtypeStruct((rows, width), bf),
            jax.ShapeDtypeStruct((n_seq,) + finished_cache.shape, bf),
            jax.ShapeDtypeStruct((n_seq, 8, slots), jnp.int32),
        ),
        in_specs=[
            vmem, vmem, anywhere, anywhere, anywhere, anywhere, vmem, vmem, smem, anywhere,
            vmem, vmem,
        ],
        out_specs=(vmem, anywhere, anywhere),
        scratch_shapes=[
            pltpu.VMEM((n_tp, rows, width), bf),
            pltpu.VMEM(q_weight.shape, bf),
            pltpu.VMEM((D, 2 * HD), bf),
            pltpu.VMEM(out_weight.shape, bf),
            pltpu.VMEM((n_seq, ctx_rows, 2 * HD), bf),
            pltpu.VMEM((n_seq, rows, 2 * HD), bf),
            pltpu.VMEM((8, slots), jnp.int32),
            pltpu.VMEM((rows, width), f32),
            pltpu.VMEM((rows, 2 * HD), f32),
            pltpu.VMEM((heads, rows, HD), bf),
            pltpu.VMEM((heads, rows, 1), f32),
            pltpu.VMEM((heads, rows, 1), f32),
            pltpu.VMEM((heads, rows, HD), f32),
            pltpu.VMEM((rows, width), bf),
            pltpu.VMEM((NZ, rows, width), bf),
            pltpu.VMEM((NZ, rows, width), bf),
            pltpu.VMEM((NZ, rows, width), bf),
            pltpu.VMEM((NZ, rows, width), bf),
            pltpu.VMEM(((n_seq,) + finished_cache.shape) if in_vmem else (8, HD), bf),
            dma((3,)),
            dma((3,)),
        ]
        + [dma((NZ,))] * 4
        + [dma((chips,))] * 16
        + [dma((NZ,))] * 4
        + [dma((n_seq,))],
        compiler_params=pltpu.CompilerParams(
            collective_id=0, has_side_effects=True, vmem_limit_bytes=56 * 1024 * 1024
        ),
        name="layer",
    )(
        tokens,
        norm_gain.reshape(n_tp, 1, width),
        q_weight,
        kv_weight.reshape(D, 2 * HD),
        out_weight,
        ctx_cache.reshape(ctx_rows, 2 * HD),
        cosf,
        sinf,
        span_start,
        finished_cache,
        block_dest,
        block_dest.reshape(1, blocks),
    )
    page_pool = pl.pallas_call(
        functools.partial(pool_kernel, n_seq, capacity),
        out_shape=jax.ShapeDtypeStruct(
            (LAYERS, slots * BLK) + finished_cache.shape[2:], bf
        ),
        in_specs=[anywhere, smem],
        out_specs=anywhere,
        scratch_shapes=[
            pltpu.VMEM((LAYERS, BLK) + finished_cache.shape[2:], bf),
            pltpu.VMEM((n_seq,) + finished_cache.shape, bf),
            dma,
            dma((n_seq,)),
        ],
        compiler_params=pltpu.CompilerParams(vmem_limit_bytes=56 * 1024 * 1024),
        name="pool",
    )(fin_all, map_all)
    return (attended, page_pool)


def solution(mesh):
    return jax.shard_map(
        functools.partial(on_device, mesh.shape["seq"], mesh.shape["tp"]),
        mesh=mesh,
        in_specs=(
            P("seq", "tp"),
            P(),
            P(None, "tp"),
            P(None, None, "tp"),
            P("tp", None),
            P("seq", None, "tp"),
            P(),
            P(None, "seq", None, "tp"),
            P("seq", None),
        ),
        out_specs=(P("seq", "tp"), P(None, "seq", None, "tp")),
        check_vma=False,
    )
```
